256 devices in a mesh: dp: 32 (over y, z), tensor: 8 (over x, core).
Axes of the slice: x: 4, y: 4, z: 8, core: 2. Of those that a mesh axis runs over, the one named last changes fastest.
Arguments:
- tree_ids: int32 [32, 64], P('dp'), may hold values from 0 to 65535, as said below
- ancestors: int32 [32, 64, 64], P('dp'), may hold values from 0 to 1, as said below
- lengths: int32 [32], P('dp'), may hold values from 64 to 1024, as said below
- table: bfloat16 [65536, 4096], P('dp', 'tensor'), may hold values from -3 to 3
- gain: bfloat16 [4096], replicated, may hold values from 0.25 to 1.75
- w_query: bfloat16 [4096, 4096], P(None, 'tensor'), may hold values from -0.09375 to 0.09375
- w_kv: bfloat16 [2, 4096, 1024], P(None, None, 'tensor'), may hold values from -0.09375 to 0.09375
- w_out: bfloat16 [4096, 4096], P('tensor'), may hold values from -0.09375 to 0.09375
- key_cache: bfloat16 [32, 8, 1024, 128], P('dp', 'tensor'), may hold values from -480 to 480
- value_cache: bfloat16 [32, 8, 1024, 128], P('dp', 'tensor'), may hold values from -6 to 6
Outputs:
- layer_output: bfloat16 [2048, 4096], P('dp', 'tensor')
The draws below stay inside these ranges and needn't reach their ends.
Inputs may be any that keep to these rules, and one draw needn't show every extreme that they name: `tree_ids`: split the vocabulary into equal consecutive parts, one for each index of dp; of the nodes of the rows of one index of dp, at most 4 have ids in any one part, and exactly 4 in some part. Row n of each row's matrix marks node n and all its ancestors in that row's tree; node 0 is the root and every other node's parent has a smaller index. `lengths`: some row has all 1024 slots live.
All inputs are finite; a program needn't handle non-finite values.
Results may differ from the reference program's by a relative error of at most 0.004.
The reference program's roundings to bfloat16 on the way count: a program that leaves them out, or rounds other values in their place, can miss the bound.
Values may be sent and summed in bfloat16 or wider, within the bound.
No kernel may reach another device: no remote copies, remote signals or barrier semaphores. Data moves between devices by JAX's collectives and lax.ppermute only.
A program may use at most 64 MiB of HBM per device.

```python
import math
import jax
import jax.numpy as jnp
from jax import lax

D = 4096
HEADS = 32
KVH = 8
HD = 128
VOCAB = 65536
NODES = 64
CTX = 1024
R_DEV = 1
ROWS = 32
TOKENS = 2048
CAP = 4
N_DP = 32


def draw_tree_ids(key, part):
    block_size = R_DEV * NODES
    part_rows = VOCAB // N_DP
    block_keys = jax.random.split(key, N_DP)

    def one_block(block_key):
        chosen_key, order_key, place_key, entry_key = jax.random.split(block_key, 4)
        chosen = jax.random.randint(chosen_key, (), 0, N_DP)
        others_index = jnp.arange(CAP * (N_DP - 1), dtype=jnp.int32) // CAP
        others_owner = others_index + (others_index >= chosen).astype(jnp.int32)
        others_owner = jax.random.permutation(order_key, others_owner)
        owners_all = jnp.concatenate([jnp.full((CAP,), chosen, jnp.int32), others_owner])
        owners_block = jax.random.permutation(place_key, owners_all[:block_size])
        entries = jax.random.randint(entry_key, (block_size,), 0, part_rows)
        return (owners_block * part_rows + entries).astype(jnp.int32)
    drawn = jax.vmap(one_block)(block_keys)
    return drawn.reshape(ROWS, NODES).astype(jnp.int32)


def draw_ancestors(key, part):
    raw_bits = jax.random.randint(key, (ROWS, NODES), 0, 2 ** 30)
    node_index = jnp.arange(NODES, dtype=jnp.int32)
    parents = raw_bits % jnp.maximum(node_index, 1)[None, :]

    def build(parent_row):
        start_matrix = jnp.zeros((NODES, NODES), jnp.int32).at[0, 0].set(1)

        def add_node(node, matrix):
            new_row = matrix[parent_row[node]].at[node].set(1)
            return matrix.at[node].set(new_row)
        return lax.fori_loop(1, NODES, add_node, start_matrix)
    return jax.vmap(build)(parents).astype(jnp.int32)


def draw_lengths(key, part):
    first_key, second_key = jax.random.split(key)
    values_drawn = jax.random.randint(first_key, (ROWS,), CTX // 16, CTX + 1)
    chosen = jax.random.randint(second_key, (), 0, ROWS)
    return jnp.where(jnp.arange(ROWS) == chosen, CTX, values_drawn).astype(jnp.int32)


def draw_key_cache(key, part):
    base_draw = jnp.clip(jax.random.normal(key, (ROWS, KVH, CTX, HD), jnp.float32), -8.0, 8.0) * 2.5
    return base_draw.astype(jnp.bfloat16)


def levels(stream_key, shape, cuts, smallest, high):
    level, own = 1.0, jax.random.fold_in(stream_key, 6)
    for position, parts in cuts:
        heights = jnp.exp(jax.random.uniform(jax.random.fold_in(own, position), (parts,), jnp.float32, smallest / len(cuts), high / len(cuts)))
        level = level * jnp.repeat(heights, shape[position] // parts).reshape([-1 if axis == position else 1 for axis in range(len(shape))])
    return level


def normal_values(key, extent, scale, limit, cuts=(), held_as=jnp.bfloat16):
    level = levels(key, extent, cuts, -0.22, 0.18) if cuts else 1.0
    array = jax.random.normal(key, extent, jnp.float32) * scale * level
    return jnp.minimum(jnp.maximum(array, -limit), limit).astype(held_as)


def setup_inputs(seed: int = 0) -> dict:
    seeds = jax.random.split(jax.random.key(seed), 11)
    return {
        "tree_ids": draw_tree_ids(jax.random.fold_in(seeds[10], 71), 0),
        "ancestors": draw_ancestors(jax.random.fold_in(seeds[10], 71), 0),
        "lengths": draw_lengths(jax.random.fold_in(seeds[10], 71), 0),
        "table": normal_values(seeds[3], (VOCAB, D), 0.5, 3.0, ((0, 32), (1, 8))),
        "gain": jnp.clip(1.0 + 0.15 * jax.random.normal(seeds[4], (D,), jnp.float32), 0.25, 1.75).astype(jnp.bfloat16),
        "w_query": normal_values(seeds[5], (D, HEADS * HD), D ** -0.5, 0.09375, ((1, 8),)),
        "w_kv": normal_values(seeds[6], (2, D, KVH * HD), D ** -0.5, 0.09375, ((2, 8),)),
        "w_out": normal_values(seeds[7], (HEADS * HD, D), (HEADS * HD) ** -0.5, 0.09375, ((0, 8),)),
        "key_cache": draw_key_cache(jax.random.fold_in(seeds[10], 71), 0),
        "value_cache": normal_values(seeds[9], (ROWS, KVH, CTX, HD), 1.0, 6.0, ((0, 32), (1, 8))),
    }


EPS = 1e-05
NEG = -1e+30
THETA = 500000.0

def rotary(values, positions):
    half_dim = values.shape[-1] // 2
    freq_index = jnp.arange(half_dim, dtype=jnp.float32)
    inverse = jnp.exp(freq_index * (-2.0 * math.log(THETA) / values.shape[-1]))
    angles = positions[:, None] * inverse[None, :]
    cosine = jnp.cos(angles)[:, None, :]
    sine_part = jnp.sin(angles)[:, None, :]
    lower_half = values[..., :half_dim]
    upper_half = values[..., half_dim:]
    return jnp.concatenate([lower_half * cosine - upper_half * sine_part, upper_half * cosine + lower_half * sine_part], axis=-1)

def contract(left_side, right_side):
    return lax.dot_general(left_side, right_side, (((1,), (1,)), ((), ())), preferred_element_type=jnp.float32)

def attend(query_group, keys_tree, values_tree, keys_cache, values_cache, live_len, tree_mask):
    score_scale = keys_cache.shape[-1] ** (-0.5)
    cache_scores = contract(query_group, keys_cache) * score_scale
    columns = jnp.arange(keys_cache.shape[0], dtype=jnp.int32)
    cache_scores = jnp.where(columns[None, :] < live_len, cache_scores, NEG)
    tree_scores = contract(query_group, keys_tree) * score_scale
    groups = query_group.shape[0] // tree_mask.shape[0]
    tree_scores = jnp.where(jnp.tile(tree_mask, (groups, 1)) > 0, tree_scores, NEG)
    row_top = jnp.maximum(lax.optimization_barrier(jnp.max(cache_scores, axis=1)), lax.optimization_barrier(jnp.max(tree_scores, axis=1)))[:, None]
    cache_exp = jnp.exp(cache_scores - row_top)
    tree_exp = jnp.exp(tree_scores - row_top)
    denominator = lax.optimization_barrier(jnp.sum(cache_exp, axis=1)) + lax.optimization_barrier(jnp.sum(tree_exp, axis=1))
    weighted = jnp.dot(cache_exp.astype(jnp.bfloat16), values_cache, preferred_element_type=jnp.float32)
    weighted = weighted + jnp.dot(tree_exp.astype(jnp.bfloat16), values_tree, preferred_element_type=jnp.float32)
    return (weighted / denominator[:, None]).astype(jnp.bfloat16)

def to_groups(tensor_in, kv_heads, head_dim):
    row_count, node_count, width_all = tensor_in.shape
    per_group = width_all // (kv_heads * head_dim)
    grouped = tensor_in.reshape(row_count, node_count, kv_heads, per_group, head_dim).transpose(0, 2, 3, 1, 4)
    return grouped.reshape(row_count, kv_heads, per_group * node_count, head_dim)

def from_groups(tensor_in, node_count):
    row_count, kv_heads, group_rows, head_dim = tensor_in.shape
    grouped = tensor_in.reshape(row_count, kv_heads, group_rows // node_count, node_count, head_dim)
    return grouped.transpose(0, 3, 1, 2, 4).reshape(row_count, node_count, -1)

def reference(tree_ids, ancestors, lengths, table, gain, w_query, w_kv, w_out, key_cache, value_cache):
    embedded = table[tree_ids.reshape(-1)]
    features = embedded.astype(jnp.float32)
    inv_rms = lax.rsqrt(lax.optimization_barrier(jnp.sum(features * features, axis=1)) / D + EPS)
    normed = (features * inv_rms[:, None] * gain.astype(jnp.float32)[None, :]).astype(jnp.bfloat16)
    queries = jnp.dot(normed, w_query, preferred_element_type=jnp.float32)
    keys_new = jnp.dot(normed, w_kv[0], preferred_element_type=jnp.float32)
    values_new = jnp.dot(normed, w_kv[1], preferred_element_type=jnp.float32).astype(jnp.bfloat16)
    node_depth = lax.optimization_barrier(jnp.sum(ancestors, axis=2)) - 1
    positions = (lengths[:, None] + node_depth).reshape(-1).astype(jnp.float32)
    queries = rotary(queries.reshape(TOKENS, HEADS, HD), positions).astype(jnp.bfloat16).reshape(ROWS, NODES, HEADS * HD)
    keys_new = rotary(keys_new.reshape(TOKENS, KVH, HD), positions).astype(jnp.bfloat16).reshape(ROWS, NODES, KVH * HD)
    values_new = values_new.reshape(ROWS, NODES, KVH * HD)
    query_groups = to_groups(queries, KVH, HD)
    key_groups = to_groups(keys_new, KVH, HD)
    value_groups = to_groups(values_new, KVH, HD)

    def per_row(row_items):
        row_q, row_k, row_v, row_kc, row_vc, live_len, tree_mask = row_items

        def per_head(head_items):
            return attend(head_items[0], head_items[1], head_items[2], head_items[3], head_items[4], live_len, tree_mask)
        return lax.map(per_head, (row_q, row_k, row_v, row_kc, row_vc))
    contexts = lax.map(per_row, (query_groups, key_groups, value_groups, key_cache, value_cache, lengths, ancestors))
    contexts = from_groups(contexts, NODES).reshape(TOKENS, HEADS * HD)
    attention = jnp.dot(contexts, w_out, preferred_element_type=jnp.float32)
    return (features + attention).astype(jnp.bfloat16)
```

```python
import functools
import math

import jax
import jax.numpy as jnp
from jax import lax
from jax.experimental import pallas as pl
from jax.experimental.pallas import tpu as pltpu
from jax.sharding import PartitionSpec as P

D = 4096
HD = 128
CAP = 4
EPS = 1e-05
NEG = -1e30
THETA = 500000.0
BF = jnp.bfloat16
F32 = jnp.float32


def iota(shape, dim):
    return lax.broadcasted_iota(jnp.int32, shape, dim)


def rows_kernel(idx_ref, ids_ref, table_ref, out_ref):
    vocab = table_ref.shape[0]
    n_dst, nodes = ids_ref.shape
    off = ids_ref[...] - idx_ref[0] * vocab
    owned = (off >= 0) & (off < vocab)
    before = jnp.where(iota((nodes, nodes), 0) < iota((nodes, nodes), 1), 1.0, 0.0).astype(BF)
    rank = jnp.dot(jnp.where(owned, 1.0, 0.0).astype(BF), before, preferred_element_type=F32)
    high = jnp.where(owned, rank * (vocab // 256) + (off >> 8).astype(F32), -1.0).astype(BF)
    low = jnp.where(owned, (off & 255).astype(F32), 0.0).astype(BF)
    n_out = n_dst * 2 * CAP
    spread = jnp.where(
        (iota((n_out, n_dst), 0) >> 3) == iota((n_out, n_dst), 1), 1.0, 0.0
    ).astype(BF)
    code = 256.0 * jnp.dot(spread, high, preferred_element_type=F32) + jnp.dot(
        spread, low, preferred_element_type=F32
    )
    code = code.astype(jnp.int32)
    slot = (iota((n_out, nodes), 0) & (CAP - 1)) * vocab
    rel = code - slot
    entry = jnp.max(
        jnp.where((rel >= 0) & (rel < vocab), rel, -1).astype(F32), axis=1, keepdims=True
    ).astype(jnp.int32)
    pick = jnp.where(iota((n_out, vocab), 1) == entry, 1.0, 0.0).astype(BF)
    rows = jnp.dot(pick, table_ref[...], preferred_element_type=F32)
    half = rows.shape[1] // 2
    upper = (iota((n_out, half), 0) & CAP) > 0
    out_ref[...] = jnp.where(upper, rows[:, half:], rows[:, :half]).astype(BF)


def pick_kernel(ids_ref, recv_ref, out_ref, *, vocab):
    nodes = ids_ref.shape[1]
    n_in, half = recv_ref.shape
    ids_row = jnp.broadcast_to(ids_ref[...], (nodes, nodes)) // vocab
    owner_row = ids_row.astype(F32)
    owner_col = owner_row.T
    same = (owner_row == owner_col) & (iota((nodes, nodes), 1) < iota((nodes, nodes), 0))
    rank = jnp.sum(jnp.where(same, 1.0, 0.0), axis=1, keepdims=True)
    slot = (owner_col[:, 0:1] * 8.0 + rank).astype(jnp.int32)
    columns = iota((nodes, n_in), 1)
    recv = recv_ref[...]
    low = jnp.where(columns == slot, 1.0, 0.0).astype(BF)
    high = jnp.where(columns == slot + CAP, 1.0, 0.0).astype(BF)
    out_ref[:, :half] = jnp.dot(low, recv, preferred_element_type=F32).astype(BF)
    out_ref[:, half:] = jnp.dot(high, recv, preferred_element_type=F32).astype(BF)


def rotate(x, cos, sin):
    return x * cos + pltpu.roll(x, HD // 2, 1) * sin


def layer_kernel(
    idx_ref, len_ref, mine_ref, other_ref, gain_ref, wq_ref, wkv_ref, wout_ref, kc_ref, vc_ref,
    anc_ref, cos_ref, sin_ref, ctx_ref, send_ref, normed,
):
    me = idx_ref[0]
    n_x, nodes, width = mine_ref.shape
    total = jnp.zeros((nodes, 1), F32)
    for j in range(n_x):
        for ref in (mine_ref, other_ref):
            piece = ref[j].astype(F32)
            total = total + jnp.sum(piece * piece, axis=1, keepdims=True)
    inv_rms = lax.rsqrt(total / D + EPS)
    for j in range(n_x):
        for c, ref in enumerate((mine_ref, other_ref)):
            owner = (me ^ (2 * j)) ^ c
            cols = pl.ds(pl.multiple_of(owner * width, width), width)
            gain = gain_ref[:, cols].astype(F32)
            normed[:, cols] = (ref[j].astype(F32) * inv_rms * gain).astype(BF)
    x = normed[...]
    queries = jnp.dot(x, wq_ref[...], preferred_element_type=F32)
    keys = jnp.dot(x, wkv_ref[0], preferred_element_type=F32)
    values = jnp.dot(x, wkv_ref[1], preferred_element_type=F32).astype(BF)
    cos = cos_ref[...]
    sin = sin_ref[...]
    heads = queries.shape[1] // HD
    keys = rotate(keys, cos, sin).astype(BF)
    group = jnp.concatenate(
        [rotate(queries[:, h * HD : (h + 1) * HD], cos, sin).astype(BF) for h in range(heads)], axis=0
    )
    contract = (((1,), (1,)), ((), ()))
    scale = HD ** (-0.5)
    slots = kc_ref.shape[0]
    s_cache = lax.dot_general(group, kc_ref[...], contract, preferred_element_type=F32) * scale
    s_cache = jnp.where(iota((1, slots), 1) < len_ref[0], s_cache, NEG)
    s_tree = lax.dot_general(group, keys, contract, preferred_element_type=F32) * scale
    mask = jnp.concatenate([anc_ref[...]] * heads, axis=0)
    s_tree = jnp.where(mask > 0, s_tree, NEG)
    top = jnp.maximum(
        jnp.max(s_cache, axis=1, keepdims=True), jnp.max(s_tree, axis=1, keepdims=True)
    )
    e_cache = jnp.exp(s_cache - top)
    e_tree = jnp.exp(s_tree - top)
    denominator = jnp.sum(e_cache, axis=1, keepdims=True) + jnp.sum(e_tree, axis=1, keepdims=True)
    weighted = jnp.dot(e_cache.astype(BF), vc_ref[...], preferred_element_type=F32)
    weighted = weighted + jnp.dot(e_tree.astype(BF), values, preferred_element_type=F32)
    ctx = (weighted / denominator).astype(BF)
    ctx = jnp.concatenate([ctx[h * nodes : (h + 1) * nodes] for h in range(heads)], axis=1)
    ctx_ref[...] = ctx
    for j in range(n_x):
        cols = pl.ds(pl.multiple_of(((me ^ (2 * j)) ^ 1) * width, width), width)
        send_ref[j] = jnp.dot(ctx, wout_ref[:, cols], preferred_element_type=F32).astype(BF)


def out_kernel(idx_ref, ctx_ref, wout_ref, out_ref):
    out_ref[0] = jnp.dot(ctx_ref[...], wout_ref[...], preferred_element_type=F32)


def swap(n, k):
    return [(i, i ^ k) for i in range(n)]


def shards(tree_ids, ancestors, lengths, table, gain, w_query, w_kv, w_out, key_cache, value_cache):
    n_dp = lax.axis_size("dp")
    n_tp = lax.axis_size("tensor")
    n_x = n_tp // 2
    nodes = tree_ids.shape[1]
    vocab, width = table.shape
    me = lax.axis_index("tensor")
    me_arr = me.astype(jnp.int32).reshape(1)
    part = lax.axis_index("dp").astype(jnp.int32).reshape(1)
    vmem = pl.BlockSpec(memory_space=pltpu.VMEM)
    smem = pl.BlockSpec(memory_space=pltpu.SMEM)

    all_ids = lax.all_gather(tree_ids, "dp", axis=0, tiled=True)
    rows = pl.pallas_call(
        rows_kernel,
        out_shape=jax.ShapeDtypeStruct((n_dp * 2 * CAP, width // 2), BF),
        in_specs=[smem, vmem, vmem],
        out_specs=vmem,
        name="rows",
    )(part, all_ids, table)
    recv = lax.all_to_all(
        rows.reshape(n_dp, 2 * CAP, width // 2), "dp", split_axis=0, concat_axis=0, tiled=True
    )
    emb = pl.pallas_call(
        functools.partial(pick_kernel, vocab=vocab),
        out_shape=jax.ShapeDtypeStruct((nodes, width), BF),
        in_specs=[vmem, vmem],
        out_specs=vmem,
        name="pick",
    )(tree_ids, recv.reshape(n_dp * 2 * CAP, width // 2))

    mine = jnp.stack(
        [emb] + [lax.ppermute(emb, "tensor", swap(n_tp, 2 * j)) for j in range(1, n_x)], 0
    )
    other = lax.ppermute(mine, "tensor", swap(n_tp, 1))

    depth = jnp.sum(ancestors[0], axis=1) - 1
    positions = (lengths[0] + depth).astype(F32)
    freq_index = jnp.arange(HD // 2, dtype=F32)
    inverse = jnp.exp(freq_index * (-2.0 * math.log(THETA) / HD))
    angles = positions[:, None] * inverse[None, :]
    cosine = jnp.cos(angles)
    sine = jnp.sin(angles)
    cos = jnp.concatenate([cosine, cosine], axis=1)
    sin = jnp.concatenate([-sine, sine], axis=1)

    ctx, send = pl.pallas_call(
        layer_kernel,
        out_shape=(
            jax.ShapeDtypeStruct((nodes, width), BF),
            jax.ShapeDtypeStruct((n_x, nodes, width), BF),
        ),
        in_specs=[smem, smem] + [vmem] * 11,
        out_specs=(vmem, vmem),
        scratch_shapes=[pltpu.VMEM((nodes, n_tp * width), BF)],
        compiler_params=pltpu.CompilerParams(vmem_limit_bytes=40 * 1024 * 1024),
        name="layer",
    )(
        me_arr, lengths, mine, other, gain.reshape(1, -1), w_query, w_kv, w_out,
        key_cache[0, 0], value_cache[0, 0], ancestors[0], cos, sin,
    )
    came = lax.ppermute(send, "tensor", swap(n_tp, 1))
    own = pl.pallas_call(
        out_kernel,
        grid_spec=pltpu.PrefetchScalarGridSpec(
            num_scalar_prefetch=1,
            grid=(n_x,),
            in_specs=[
                pl.BlockSpec((nodes, width), lambda j, m: (0, 0)),
                pl.BlockSpec((width, width), lambda j, m: (0, m[0] ^ (2 * j))),
            ],
            out_specs=pl.BlockSpec((1, nodes, width), lambda j, m: (j, 0, 0)),
        ),
        out_shape=jax.ShapeDtypeStruct((n_x, nodes, width), F32),
        cost_estimate=pl.CostEstimate(
            flops=2 * nodes * width * width * n_x, bytes_accessed=2 * width * width * n_x, transcendentals=0
        ),
        name="project",
    )(me_arr, ctx, w_out)
    pair = own + came.astype(F32)
    attention = pair[0]
    for j in range(1, n_x):
        attention = attention + lax.ppermute(
            pair[j].astype(BF), "tensor", swap(n_tp, 2 * j)
        ).astype(F32)
    return (emb.astype(F32) + attention).astype(BF)


def solution(mesh):
    in_specs = (
        P("dp", None),
        P("dp", None, None),
        P("dp"),
        P("dp", "tensor"),
        P(),
        P(None, "tensor"),
        P(None, None, "tensor"),
        P("tensor", None),
        P("dp", "tensor", None, None),
        P("dp", "tensor", None, None),
    )
    out_specs = P("dp", "tensor")
    return jax.shard_map(shards, mesh=mesh, in_specs=in_specs, out_specs=out_specs, check_vma=False)
```

```python
import functools
import math

import jax
import jax.numpy as jnp
from jax import lax
from jax.experimental import pallas as pl
from jax.experimental.pallas import tpu as pltpu
from jax.sharding import PartitionSpec as P

D = 4096
HD = 128
CAP = 4
EPS = 1e-05
NEG = -1e30
THETA = 500000.0
BF = jnp.bfloat16
F32 = jnp.float32


def iota(shape, dim):
    return lax.broadcasted_iota(jnp.int32, shape, dim)


def rows_kernel(idx_ref, ids_ref, table_ref, out_ref):
    vocab = table_ref.shape[0]
    n_dst, nodes = ids_ref.shape
    off = ids_ref[...] - idx_ref[0] * vocab
    owned = (off >= 0) & (off < vocab)
    before = jnp.where(iota((nodes, nodes), 0) < iota((nodes, nodes), 1), 1.0, 0.0).astype(BF)
    rank = jnp.dot(jnp.where(owned, 1.0, 0.0).astype(BF), before, preferred_element_type=F32)
    high = jnp.where(owned, rank * (vocab // 256) + (off >> 8).astype(F32), -1.0).astype(BF)
    low = jnp.where(owned, (off & 255).astype(F32), 0.0).astype(BF)
    n_out = n_dst * 2 * CAP
    spread = jnp.where(
        (iota((n_out, n_dst), 0) >> 3) == iota((n_out, n_dst), 1), 1.0, 0.0
    ).astype(BF)
    code = 256.0 * jnp.dot(spread, high, preferred_element_type=F32) + jnp.dot(
        spread, low, preferred_element_type=F32
    )
    code = code.astype(jnp.int32)
    slot = (iota((n_out, nodes), 0) & (CAP - 1)) * vocab
    rel = code - slot
    entry = jnp.max(
        jnp.where((rel >= 0) & (rel < vocab), rel, -1).astype(F32), axis=1, keepdims=True
    ).astype(jnp.int32)
    pick = jnp.where(iota((n_out, vocab), 1) == entry, 1.0, 0.0).astype(BF)
    rows = jnp.dot(pick, table_ref[...], preferred_element_type=F32)
    half = rows.shape[1] // 2
    upper = (iota((n_out, half), 0) & CAP) > 0
    out_ref[...] = jnp.where(upper, rows[:, half:], rows[:, :half]).astype(BF)


def pick_kernel(ids_ref, recv_ref, out_ref, *, vocab):
    nodes = ids_ref.shape[1]
    n_in, half = recv_ref.shape
    ids_row = jnp.broadcast_to(ids_ref[...], (nodes, nodes)) // vocab
    owner_row = ids_row.astype(F32)
    owner_col = owner_row.T
    same = (owner_row == owner_col) & (iota((nodes, nodes), 1) < iota((nodes, nodes), 0))
    rank = jnp.sum(jnp.where(same, 1.0, 0.0), axis=1, keepdims=True)
    slot = (owner_col[:, 0:1] * 8.0 + rank).astype(jnp.int32)
    columns = iota((nodes, n_in), 1)
    recv = recv_ref[...]
    low = jnp.where(columns == slot, 1.0, 0.0).astype(BF)
    high = jnp.where(columns == slot + CAP, 1.0, 0.0).astype(BF)
    out_ref[:, :half] = jnp.dot(low, recv, preferred_element_type=F32).astype(BF)
    out_ref[:, half:] = jnp.dot(high, recv, preferred_element_type=F32).astype(BF)


def rotate(x, cos, sin):
    return x * cos + pltpu.roll(x, HD // 2, 1) * sin


def layer_kernel(
    idx_ref, len_ref, mine_ref, other_ref, gain_ref, wq_ref, wkv_ref, wout_ref, kc_ref, vc_ref,
    anc_ref, cos_ref, sin_ref, ctx_ref, send_ref, normed,
):
    me = idx_ref[0]
    n_x, nodes, width = mine_ref.shape
    total = jnp.zeros((nodes, 1), F32)
    for j in range(n_x):
        for ref in (mine_ref, other_ref):
            piece = ref[j].astype(F32)
            total = total + jnp.sum(piece * piece, axis=1, keepdims=True)
    inv_rms = lax.rsqrt(total / D + EPS)
    for j in range(n_x):
        for c, ref in enumerate((mine_ref, other_ref)):
            owner = (me ^ (2 * j)) ^ c
            cols = pl.ds(pl.multiple_of(owner * width, width), width)
            gain = gain_ref[:, cols].astype(F32)
            normed[:, cols] = (ref[j].astype(F32) * inv_rms * gain).astype(BF)
    x = normed[...]
    queries = jnp.dot(x, wq_ref[...], preferred_element_type=F32)
    keys = jnp.dot(x, wkv_ref[0], preferred_element_type=F32)
    values = jnp.dot(x, wkv_ref[1], preferred_element_type=F32).astype(BF)
    cos = cos_ref[...]
    sin = sin_ref[...]
    heads = queries.shape[1] // HD
    keys = rotate(keys, cos, sin).astype(BF)
    group = jnp.concatenate(
        [rotate(queries[:, h * HD : (h + 1) * HD], cos, sin).astype(BF) for h in range(heads)], axis=0
    )
    contract = (((1,), (1,)), ((), ()))
    scale = HD ** (-0.5)
    slots = kc_ref.shape[0]
    s_cache = lax.dot_general(group, kc_ref[...], contract, preferred_element_type=F32) * scale
    s_cache = jnp.where(iota((1, slots), 1) < len_ref[0], s_cache, NEG)
    s_tree = lax.dot_general(group, keys, contract, preferred_element_type=F32) * scale
    mask = jnp.concatenate([anc_ref[...]] * heads, axis=0)
    s_tree = jnp.where(mask > 0, s_tree, NEG)
    top = jnp.maximum(
        jnp.max(s_cache, axis=1, keepdims=True), jnp.max(s_tree, axis=1, keepdims=True)
    )
    e_cache = jnp.exp(s_cache - top)
    e_tree = jnp.exp(s_tree - top)
    denominator = jnp.sum(e_cache, axis=1, keepdims=True) + jnp.sum(e_tree, axis=1, keepdims=True)
    weighted = jnp.dot(e_cache.astype(BF), vc_ref[...], preferred_element_type=F32)
    weighted = weighted + jnp.dot(e_tree.astype(BF), values, preferred_element_type=F32)
    ctx = (weighted / denominator).astype(BF)
    ctx = jnp.concatenate([ctx[h * nodes : (h + 1) * nodes] for h in range(heads)], axis=1)
    ctx_ref[...] = ctx
    for j in range(n_x):
        cols = pl.ds(pl.multiple_of(((me ^ (2 * j)) ^ 1) * width, width), width)
        send_ref[j] = jnp.dot(ctx, wout_ref[:, cols], preferred_element_type=F32).astype(BF)


def load_kernel(count, *refs):
    dst = refs[-1 - count : -1]
    copies = [pltpu.make_async_copy(refs[i], dst[i], refs[-1].at[i]) for i in range(count)]
    for copy in copies:
        copy.start()
    for copy in copies:
        copy.wait()


def load(arrays, after, mib):
    return pl.pallas_call(
        functools.partial(load_kernel, len(arrays)),
        out_shape=tuple(jax.ShapeDtypeStruct(a.shape, a.dtype) for a in arrays),
        in_specs=[pl.BlockSpec(memory_space=pltpu.HBM)] * len(arrays)
        + [pl.BlockSpec(memory_space=pl.ANY)] * len(after),
        out_specs=(pl.BlockSpec(memory_space=pltpu.VMEM),) * len(arrays),
        scratch_shapes=[pltpu.SemaphoreType.DMA((len(arrays),))],
        cost_estimate=pl.CostEstimate(
            flops=0, bytes_accessed=sum(a.size * a.dtype.itemsize for a in arrays), transcendentals=0
        ),
        compiler_params=limit(mib),
        name="load",
    )(*arrays, *after)


def out_kernel(idx_ref, ctx_ref, wout_ref, out_ref):
    n_x, _, width = out_ref.shape
    ctx = ctx_ref[...]
    for j in range(n_x):
        cols = pl.ds(pl.multiple_of((idx_ref[0] ^ (2 * j)) * width, width), width)
        out_ref[j] = jnp.dot(ctx, wout_ref[:, cols], preferred_element_type=F32)


def pair_kernel(own_ref, came_ref, *out_refs):
    for j, ref in enumerate(out_refs):
        ref[...] = (own_ref[j] + came_ref[j].astype(F32)).astype(ref.dtype)


def stack_kernel(*refs):
    out_ref = refs[-1]
    for j in range(out_ref.shape[0]):
        out_ref[j] = refs[j][...]


def final_kernel(emb_ref, own_ref, *refs):
    total = own_ref[...]
    for ref in refs[:-1]:
        total = total + ref[...].astype(F32)
    refs[-1][...] = (emb_ref[...].astype(F32) + total).astype(BF)


def limit(mib):
    return pltpu.CompilerParams(vmem_limit_bytes=mib * 1024 * 1024)


def swap(n, k):
    return [(i, i ^ k) for i in range(n)]


def shards(tree_ids, ancestors, lengths, table, gain, w_query, w_kv, w_out, key_cache, value_cache):
    n_dp = lax.axis_size("dp")
    n_tp = lax.axis_size("tensor")
    n_x = n_tp // 2
    nodes = tree_ids.shape[1]
    vocab, width = table.shape
    me = lax.axis_index("tensor")
    me_arr = me.astype(jnp.int32).reshape(1)
    part = lax.axis_index("dp").astype(jnp.int32).reshape(1)
    vmem = pl.BlockSpec(memory_space=pltpu.VMEM)
    smem = pl.BlockSpec(memory_space=pltpu.SMEM)

    all_ids = lax.all_to_all(
        jnp.broadcast_to(tree_ids, (n_dp, nodes)), "dp", split_axis=0, concat_axis=0, tiled=True
    )
    (table_held,) = load((table,), (), 50)
    rows = pl.pallas_call(
        rows_kernel,
        out_shape=jax.ShapeDtypeStruct((n_dp * 2 * CAP, width // 2), BF),
        in_specs=[smem, vmem, vmem],
        out_specs=vmem,
        compiler_params=limit(12),
        name="rows",
    )(part, all_ids, table_held)
    recv = lax.all_to_all(
        rows.reshape(n_dp, 2 * CAP, width // 2), "dp", split_axis=0, concat_axis=0, tiled=True
    )
    emb = pl.pallas_call(
        functools.partial(pick_kernel, vocab=vocab),
        out_shape=jax.ShapeDtypeStruct((nodes, width), BF),
        in_specs=[vmem, vmem],
        out_specs=vmem,
        compiler_params=limit(4),
        name="pick",
    )(tree_ids, recv.reshape(n_dp * 2 * CAP, width // 2))

    w_query, w_kv, w_out = load((w_query, w_kv, w_out), (emb,), 41)
    mine = pl.pallas_call(
        stack_kernel,
        in_specs=[vmem] * n_x + [pl.BlockSpec(memory_space=pl.ANY)],
        out_specs=vmem,
        out_shape=jax.ShapeDtypeStruct((n_x, nodes, width), BF),
        compiler_params=limit(4),
        name="stack",
    )(emb, *[lax.ppermute(emb, "tensor", swap(n_tp, 2 * j)) for j in range(1, n_x)], w_kv)
    other = lax.ppermute(mine, "tensor", swap(n_tp, 1))

    depth = jnp.sum(ancestors[0], axis=1) - 1
    positions = (lengths[0] + depth).astype(F32)
    freq_index = jnp.arange(HD // 2, dtype=F32)
    inverse = jnp.exp(freq_index * (-2.0 * math.log(THETA) / HD))
    angles = positions[:, None] * inverse[None, :]
    cosine = jnp.cos(angles)
    sine = jnp.sin(angles)
    cos = jnp.concatenate([cosine, cosine], axis=1)
    sin = jnp.concatenate([-sine, sine], axis=1)

    ctx, send = pl.pallas_call(
        layer_kernel,
        out_shape=(
            jax.ShapeDtypeStruct((nodes, width), BF),
            jax.ShapeDtypeStruct((n_x, nodes, width), BF),
        ),
        in_specs=[smem, smem] + [vmem] * 11,
        out_specs=(vmem, vmem),
        scratch_shapes=[pltpu.VMEM((nodes, n_tp * width), BF)],
        compiler_params=limit(16),
        name="layer",
    )(
        me_arr, lengths, mine, other, gain.reshape(1, -1), w_query, w_kv, w_out,
        key_cache[0, 0], value_cache[0, 0], ancestors[0], cos, sin,
    )
    came = lax.ppermute(send, "tensor", swap(n_tp, 1))
    own = pl.pallas_call(
        out_kernel,
        in_specs=[smem, vmem, vmem],
        out_specs=vmem,
        out_shape=jax.ShapeDtypeStruct((n_x, nodes, width), F32),
        cost_estimate=pl.CostEstimate(
            flops=2 * nodes * width * width * n_x, bytes_accessed=2 * width * width * n_x, transcendentals=0
        ),
        compiler_params=limit(8),
        name="project",
    )(me_arr, ctx, w_out)
    pairs = pl.pallas_call(
        pair_kernel,
        in_specs=[vmem, vmem],
        out_specs=(vmem,) * n_x,
        out_shape=tuple(jax.ShapeDtypeStruct((nodes, width), F32 if j == 0 else BF) for j in range(n_x)),
        compiler_params=limit(4),
        name="pair",
    )(own, came)
    parts = [lax.ppermute(pairs[j], "tensor", swap(n_tp, 2 * j)) for j in range(1, n_x)]
    return pl.pallas_call(
        final_kernel,
        in_specs=[vmem] * (n_x + 1),
        out_specs=vmem,
        out_shape=jax.ShapeDtypeStruct((nodes, width), BF),
        compiler_params=limit(4),
        name="final",
    )(emb, pairs[0], *parts)


def solution(mesh):
    in_specs = (
        P("dp", None),
        P("dp", None, None),
        P("dp"),
        P("dp", "tensor"),
        P(),
        P(None, "tensor"),
        P(None, None, "tensor"),
        P("tensor", None),
        P("dp", "tensor", None, None),
        P("dp", "tensor", None, None),
    )
    out_specs = P("dp", "tensor")
    return jax.shard_map(shards, mesh=mesh, in_specs=in_specs, out_specs=out_specs, check_vma=False)
```

```python
import functools
import math

import jax
import jax.numpy as jnp
from jax import lax
from jax.experimental import pallas as pl
from jax.experimental.pallas import tpu as pltpu
from jax.sharding import PartitionSpec as P

D = 4096
HD = 128
CAP = 4
EPS = 1e-05
NEG = -1e30
THETA = 500000.0
BF = jnp.bfloat16
F32 = jnp.float32


def iota(shape, dim):
    return lax.broadcasted_iota(jnp.int32, shape, dim)


def rows_kernel(idx_ref, ids_ref, table_ref, out_ref):
    vocab = table_ref.shape[0]
    n_dst, nodes = ids_ref.shape
    off = ids_ref[...] - idx_ref[0] * vocab
    owned = (off >= 0) & (off < vocab)
    before = jnp.where(iota((nodes, nodes), 0) < iota((nodes, nodes), 1), 1.0, 0.0).astype(BF)
    rank = jnp.dot(jnp.where(owned, 1.0, 0.0).astype(BF), before, preferred_element_type=F32)
    high = jnp.where(owned, rank * (vocab // 256) + (off >> 8).astype(F32), -1.0).astype(BF)
    low = jnp.where(owned, (off & 255).astype(F32), 0.0).astype(BF)
    n_out = n_dst * CAP
    spread = jnp.where(
        iota((n_out, n_dst), 0) // CAP == iota((n_out, n_dst), 1), 1.0, 0.0
    ).astype(BF)
    code = 256.0 * jnp.dot(spread, high, preferred_element_type=F32) + jnp.dot(
        spread, low, preferred_element_type=F32
    )
    code = code.astype(jnp.int32)
    slot = (iota((n_out, nodes), 0) & (CAP - 1)) * vocab
    rel = code - slot
    entry = jnp.max(
        jnp.where((rel >= 0) & (rel < vocab), rel, -1).astype(F32), axis=1, keepdims=True
    ).astype(jnp.int32)
    pick = jnp.where(iota((n_out, vocab), 1) == entry, 1.0, 0.0).astype(BF)
    rows = jnp.dot(pick, table_ref[...], preferred_element_type=F32)
    half = rows.shape[1] // 2
    low_half = rows[:, :half].reshape(n_dst // 2, 2 * CAP, half)
    high_half = rows[:, half:].reshape(n_dst // 2, 2 * CAP, half)
    first = iota(low_half.shape, 1) < CAP
    out_ref[:, 0] = jnp.where(first, low_half, pltpu.roll(high_half, CAP, 1)).astype(BF)
    out_ref[:, 1] = jnp.where(first, pltpu.roll(low_half, CAP, 1), high_half).astype(BF)


def pick_kernel(ids_ref, recv_ref, _, out_ref, *, vocab):
    nodes = ids_ref.shape[1]
    n_in, half = recv_ref.shape
    ids_row = jnp.broadcast_to(ids_ref[...], (nodes, nodes)) // vocab
    owner_row = ids_row.astype(F32)
    owner_col = owner_row.T
    same = (owner_row == owner_col) & (iota((nodes, nodes), 1) < iota((nodes, nodes), 0))
    rank = jnp.sum(jnp.where(same, 1.0, 0.0), axis=1, keepdims=True)
    slot = (owner_col[:, 0:1] * 8.0 + rank).astype(jnp.int32)
    columns = iota((nodes, n_in), 1)
    recv = recv_ref[...]
    low = jnp.where(columns == slot, 1.0, 0.0).astype(BF)
    high = jnp.where(columns == slot + CAP, 1.0, 0.0).astype(BF)
    out_ref[:, :half] = jnp.dot(low, recv, preferred_element_type=F32).astype(BF)
    out_ref[:, half:] = jnp.dot(high, recv, preferred_element_type=F32).astype(BF)


def rotate(x, cos, sin):
    return x * cos + pltpu.roll(x, HD // 2, 1) * sin


def layer_kernel(
    idx_ref, len_ref, mine_ref, other_ref, gain_ref, wq_ref, wkv_ref, wout_ref, kc_ref, vc_ref,
    anc_ref, cos_ref, sin_ref, ctx_ref, send_ref, normed,
):
    me = idx_ref[0]
    n_x, nodes, width = mine_ref.shape
    total = jnp.zeros((nodes, 1), F32)
    for j in range(n_x):
        for ref in (mine_ref, other_ref):
            piece = ref[j].astype(F32)
            total = total + jnp.sum(piece * piece, axis=1, keepdims=True)
    inv_rms = lax.rsqrt(total / D + EPS)
    for j in range(n_x):
        for c, ref in enumerate((mine_ref, other_ref)):
            owner = (me ^ (2 * j)) ^ c
            cols = pl.ds(pl.multiple_of(owner * width, width), width)
            gain = gain_ref[:, cols].astype(F32)
            normed[:, cols] = (ref[j].astype(F32) * inv_rms * gain).astype(BF)
    x = normed[...]
    queries = jnp.dot(x, wq_ref[...], preferred_element_type=F32)
    keys = jnp.dot(x, wkv_ref[0], preferred_element_type=F32)
    values = jnp.dot(x, wkv_ref[1], preferred_element_type=F32).astype(BF)
    cos = cos_ref[...]
    sin = sin_ref[...]
    heads = queries.shape[1] // HD
    keys = rotate(keys, cos, sin).astype(BF)
    group = jnp.concatenate(
        [rotate(queries[:, h * HD : (h + 1) * HD], cos, sin).astype(BF) for h in range(heads)], axis=0
    )
    contract = (((1,), (1,)), ((), ()))
    scale = HD ** (-0.5)
    slots = kc_ref.shape[0]
    s_cache = lax.dot_general(group, kc_ref[...], contract, preferred_element_type=F32) * scale
    s_cache = jnp.where(iota((1, slots), 1) < len_ref[0], s_cache, NEG)
    s_tree = lax.dot_general(group, keys, contract, preferred_element_type=F32) * scale
    mask = jnp.concatenate([anc_ref[...]] * heads, axis=0)
    s_tree = jnp.where(mask > 0, s_tree, NEG)
    top = jnp.maximum(
        jnp.max(s_cache, axis=1, keepdims=True), jnp.max(s_tree, axis=1, keepdims=True)
    )
    e_cache = jnp.exp(s_cache - top)
    e_tree = jnp.exp(s_tree - top)
    denominator = jnp.sum(e_cache, axis=1, keepdims=True) + jnp.sum(e_tree, axis=1, keepdims=True)
    weighted = jnp.dot(e_cache.astype(BF), vc_ref[...], preferred_element_type=F32)
    weighted = weighted + jnp.dot(e_tree.astype(BF), values, preferred_element_type=F32)
    ctx = (weighted / denominator).astype(BF)
    ctx = jnp.concatenate([ctx[h * nodes : (h + 1) * nodes] for h in range(heads)], axis=1)
    ctx_ref[...] = ctx
    for j in range(n_x):
        cols = pl.ds(pl.multiple_of(((me ^ (2 * j)) ^ 1) * width, width), width)
        send_ref[j] = jnp.dot(ctx, wout_ref[:, cols], preferred_element_type=F32).astype(BF)


def spread_kernel(ids_ref, out_ref):
    out_ref[...] = jnp.broadcast_to(ids_ref[...], out_ref.shape)


def load_kernel(count, *refs):
    dst = refs[-1 - count : -1]
    copies = [pltpu.make_async_copy(refs[i], dst[i], refs[-1].at[i]) for i in range(count)]
    for copy in copies:
        copy.start()
    for copy in copies:
        copy.wait()


def load(arrays, after, mib):
    return pl.pallas_call(
        functools.partial(load_kernel, len(arrays)),
        out_shape=tuple(jax.ShapeDtypeStruct(a.shape, a.dtype) for a in arrays),
        in_specs=[pl.BlockSpec(memory_space=pltpu.HBM)] * len(arrays)
        + [pl.BlockSpec(memory_space=pl.ANY)] * len(after),
        out_specs=(pl.BlockSpec(memory_space=pltpu.VMEM),) * len(arrays),
        scratch_shapes=[pltpu.SemaphoreType.DMA((len(arrays),))],
        cost_estimate=pl.CostEstimate(
            flops=0, bytes_accessed=sum(a.size * a.dtype.itemsize for a in arrays), transcendentals=0
        ),
        compiler_params=limit(mib),
        name="load",
    )(*arrays, *after)


def out_kernel(idx_ref, ctx_ref, wout_ref, out_ref):
    n_x, _, width = out_ref.shape
    ctx = ctx_ref[...]
    for j in range(n_x):
        cols = pl.ds(pl.multiple_of((idx_ref[0] ^ (2 * j)) * width, width), width)
        out_ref[j] = jnp.dot(ctx, wout_ref[:, cols], preferred_element_type=F32)


def pair_kernel(own_ref, came_ref, *out_refs):
    for j, ref in enumerate(out_refs):
        ref[...] = (own_ref[j] + came_ref[j].astype(F32)).astype(ref.dtype)


def stack_kernel(*refs):
    out_ref = refs[-1]
    for j in range(out_ref.shape[0]):
        out_ref[j] = refs[j][...]


def final_kernel(emb_ref, own_ref, *refs):
    total = own_ref[...]
    for ref in refs[:-1]:
        total = total + ref[...].astype(F32)
    refs[-1][...] = (emb_ref[...].astype(F32) + total).astype(BF)


def limit(mib):
    return pltpu.CompilerParams(vmem_limit_bytes=mib * 1024 * 1024)


def swap(n, k):
    return [(i, i ^ k) for i in range(n)]


def shards(tree_ids, ancestors, lengths, table, gain, w_query, w_kv, w_out, key_cache, value_cache):
    n_dp = lax.axis_size("dp")
    n_tp = lax.axis_size("tensor")
    n_x = n_tp // 2
    nodes = tree_ids.shape[1]
    vocab, width = table.shape
    me = lax.axis_index("tensor")
    me_arr = me.astype(jnp.int32).reshape(1)
    part = lax.axis_index("dp").astype(jnp.int32).reshape(1)
    vmem = pl.BlockSpec(memory_space=pltpu.VMEM)
    smem = pl.BlockSpec(memory_space=pltpu.SMEM)

    copies = pl.pallas_call(
        spread_kernel,
        out_shape=jax.ShapeDtypeStruct((n_dp, nodes), jnp.int32),
        in_specs=[vmem],
        out_specs=vmem,
        compiler_params=limit(60),
        name="spread",
    )(tree_ids)
    all_ids = lax.all_to_all(copies, "dp", split_axis=0, concat_axis=0, tiled=True)
    (table_held,) = load((table,), (), 50)
    rows = pl.pallas_call(
        rows_kernel,
        out_shape=jax.ShapeDtypeStruct((n_dp // 2, 2, 2 * CAP, width // 2), BF),
        in_specs=[smem, vmem, vmem],
        out_specs=vmem,
        compiler_params=limit(12),
        name="rows",
    )(part, all_ids, table_held)
    w_kv, key_cache, value_cache = load((w_kv, key_cache, value_cache), (rows,), 50)
    recv = lax.all_to_all(
        rows.reshape(n_dp, 2 * CAP, width // 2), "dp", split_axis=0, concat_axis=0, tiled=True
    )
    emb = pl.pallas_call(
        functools.partial(pick_kernel, vocab=vocab),
        out_shape=jax.ShapeDtypeStruct((nodes, width), BF),
        in_specs=[vmem, vmem, pl.BlockSpec(memory_space=pl.ANY)],
        out_specs=vmem,
        compiler_params=limit(4),
        name="pick",
    )(tree_ids, recv.reshape(n_dp * 2 * CAP, width // 2), w_kv)

    w_query, w_out = load((w_query, w_out), (emb,), 45)
    mine = pl.pallas_call(
        stack_kernel,
        in_specs=[vmem] * n_x + [pl.BlockSpec(memory_space=pl.ANY)],
        out_specs=vmem,
        out_shape=jax.ShapeDtypeStruct((n_x, nodes, width), BF),
        compiler_params=limit(4),
        name="stack",
    )(emb, *[lax.ppermute(emb, "tensor", swap(n_tp, 2 * j)) for j in range(1, n_x)], w_query)
    other = lax.ppermute(mine, "tensor", swap(n_tp, 1))

    depth = jnp.sum(ancestors[0], axis=1) - 1
    positions = (lengths[0] + depth).astype(F32)
    freq_index = jnp.arange(HD // 2, dtype=F32)
    inverse = jnp.exp(freq_index * (-2.0 * math.log(THETA) / HD))
    angles = positions[:, None] * inverse[None, :]
    cosine = jnp.cos(angles)
    sine = jnp.sin(angles)
    cos = jnp.concatenate([cosine, cosine], axis=1)
    sin = jnp.concatenate([-sine, sine], axis=1)

    ctx, send = pl.pallas_call(
        layer_kernel,
        out_shape=(
            jax.ShapeDtypeStruct((nodes, width), BF),
            jax.ShapeDtypeStruct((n_x, nodes, width), BF),
        ),
        in_specs=[smem, smem] + [vmem] * 11,
        out_specs=(vmem, vmem),
        scratch_shapes=[pltpu.VMEM((nodes, n_tp * width), BF)],
        compiler_params=limit(16),
        name="layer",
    )(
        me_arr, lengths, mine, other, gain.reshape(1, -1), w_query, w_kv, w_out,
        key_cache[0, 0], value_cache[0, 0], ancestors[0], cos, sin,
    )
    came = lax.ppermute(send, "tensor", swap(n_tp, 1))
    own = pl.pallas_call(
        out_kernel,
        in_specs=[smem, vmem, vmem],
        out_specs=vmem,
        out_shape=jax.ShapeDtypeStruct((n_x, nodes, width), F32),
        cost_estimate=pl.CostEstimate(
            flops=2 * nodes * width * width * n_x, bytes_accessed=2 * width * width * n_x, transcendentals=0
        ),
        compiler_params=limit(8),
        name="project",
    )(me_arr, ctx, w_out)
    pairs = pl.pallas_call(
        pair_kernel,
        in_specs=[vmem, vmem],
        out_specs=(vmem,) * n_x,
        out_shape=tuple(jax.ShapeDtypeStruct((nodes, width), F32 if j == 0 else BF) for j in range(n_x)),
        compiler_params=limit(4),
        name="pair",
    )(own, came)
    parts = [lax.ppermute(pairs[j], "tensor", swap(n_tp, 2 * j)) for j in range(1, n_x)]
    return pl.pallas_call(
        final_kernel,
        in_specs=[vmem] * (n_x + 1),
        out_specs=vmem,
        out_shape=jax.ShapeDtypeStruct((nodes, width), BF),
        compiler_params=limit(4),
        name="final",
    )(emb, pairs[0], *parts)


def solution(mesh):
    in_specs = (
        P("dp", None),
        P("dp", None, None),
        P("dp"),
        P("dp", "tensor"),
        P(),
        P(None, "tensor"),
        P(None, None, "tensor"),
        P("tensor", None),
        P("dp", "tensor", None, None),
        P("dp", "tensor", None, None),
    )
    out_specs = P("dp", "tensor")
    return jax.shard_map(shards, mesh=mesh, in_specs=in_specs, out_specs=out_specs, check_vma=False)
```

```python
import functools
import math

import jax
import jax.numpy as jnp
from jax import lax
from jax.experimental import pallas as pl
from jax.experimental.pallas import tpu as pltpu
from jax.sharding import PartitionSpec as P

D = 4096
HD = 128
CAP = 4
EPS = 1e-05
NEG = -1e30
THETA = 500000.0
BF = jnp.bfloat16
F32 = jnp.float32


def iota(shape, dim):
    return lax.broadcasted_iota(jnp.int32, shape, dim)


def rows_kernel(idx_ref, ids_ref, table_ref, out_ref):
    vocab = table_ref.shape[0]
    n_dst, nodes = ids_ref.shape
    off = ids_ref[...] - idx_ref[0] * vocab
    owned = (off >= 0) & (off < vocab)
    before = jnp.where(iota((nodes, nodes), 0) < iota((nodes, nodes), 1), 1.0, 0.0).astype(BF)
    rank = jnp.dot(jnp.where(owned, 1.0, 0.0).astype(BF), before, preferred_element_type=F32)
    high = jnp.where(owned, rank * (vocab // 256) + (off >> 8).astype(F32), -1.0).astype(BF)
    low = jnp.where(owned, (off & 255).astype(F32), 0.0).astype(BF)
    n_out = n_dst * CAP
    spread = jnp.where(
        iota((n_out, n_dst), 0) // CAP == iota((n_out, n_dst), 1), 1.0, 0.0
    ).astype(BF)
    code = 256.0 * jnp.dot(spread, high, preferred_element_type=F32) + jnp.dot(
        spread, low, preferred_element_type=F32
    )
    code = code.astype(jnp.int32)
    slot = (iota((n_out, nodes), 0) & (CAP - 1)) * vocab
    rel = code - slot
    entry = jnp.max(
        jnp.where((rel >= 0) & (rel < vocab), rel, -1).astype(F32), axis=1, keepdims=True
    ).astype(jnp.int32)
    pick = jnp.where(iota((n_out, vocab), 1) == entry, 1.0, 0.0).astype(BF)
    rows = jnp.dot(pick, table_ref[...], preferred_element_type=F32)
    half = rows.shape[1] // 2
    low_half = rows[:, :half].reshape(n_dst // 2, 2 * CAP, half)
    high_half = rows[:, half:].reshape(n_dst // 2, 2 * CAP, half)
    first = iota(low_half.shape, 1) < CAP
    out_ref[:, 0] = jnp.where(first, low_half, pltpu.roll(high_half, CAP, 1)).astype(BF)
    out_ref[:, 1] = jnp.where(first, pltpu.roll(low_half, CAP, 1), high_half).astype(BF)


def pick_kernel(ids_ref, recv_ref, _, out_ref, *, vocab):
    nodes = ids_ref.shape[1]
    n_in, half = recv_ref.shape
    ids_row = jnp.broadcast_to(ids_ref[...], (nodes, nodes)) // vocab
    owner_row = ids_row.astype(F32)
    owner_col = owner_row.T
    same = (owner_row == owner_col) & (iota((nodes, nodes), 1) < iota((nodes, nodes), 0))
    rank = jnp.sum(jnp.where(same, 1.0, 0.0), axis=1, keepdims=True)
    slot = (owner_col[:, 0:1] * 8.0 + rank).astype(jnp.int32)
    columns = iota((nodes, n_in), 1)
    recv = recv_ref[...]
    low = jnp.where(columns == slot, 1.0, 0.0).astype(BF)
    high = jnp.where(columns == slot + CAP, 1.0, 0.0).astype(BF)
    out_ref[:, :half] = jnp.dot(low, recv, preferred_element_type=F32).astype(BF)
    out_ref[:, half:] = jnp.dot(high, recv, preferred_element_type=F32).astype(BF)


def step(j, device):
    core = device & 1
    return device ^ (0, 2 + 2 * core, 4 + 2 * core, 6 - 4 * core)[j]


def rotate(x, cos, sin):
    return x * cos + pltpu.roll(x, HD // 2, 1) * sin


def layer_kernel(
    idx_ref, len_ref, mine_ref, other_ref, gain_ref, wq_ref, wkv_ref, wout_ref, kc_ref, vc_ref,
    anc_ref, cos_ref, sin_ref, ctx_ref, send_ref, normed,
):
    me = idx_ref[0]
    n_x, nodes, width = mine_ref.shape
    total = jnp.zeros((nodes, 1), F32)
    for j in range(n_x):
        for ref in (mine_ref, other_ref):
            piece = ref[j].astype(F32)
            total = total + jnp.sum(piece * piece, axis=1, keepdims=True)
    inv_rms = lax.rsqrt(total / D + EPS)
    for j in range(n_x):
        for c, ref in enumerate((mine_ref, other_ref)):
            owner = step(j, me ^ c)
            cols = pl.ds(pl.multiple_of(owner * width, width), width)
            gain = gain_ref[:, cols].astype(F32)
            normed[:, cols] = (ref[j].astype(F32) * inv_rms * gain).astype(BF)
    x = normed[...]
    queries = jnp.dot(x, wq_ref[...], preferred_element_type=F32)
    keys = jnp.dot(x, wkv_ref[0], preferred_element_type=F32)
    values = jnp.dot(x, wkv_ref[1], preferred_element_type=F32).astype(BF)
    cos = cos_ref[...]
    sin = sin_ref[...]
    heads = queries.shape[1] // HD
    keys = rotate(keys, cos, sin).astype(BF)
    group = jnp.concatenate(
        [rotate(queries[:, h * HD : (h + 1) * HD], cos, sin).astype(BF) for h in range(heads)], axis=0
    )
    contract = (((1,), (1,)), ((), ()))
    scale = HD ** (-0.5)
    slots = kc_ref.shape[0]
    s_cache = lax.dot_general(group, kc_ref[...], contract, preferred_element_type=F32) * scale
    s_cache = jnp.where(iota((1, slots), 1) < len_ref[0], s_cache, NEG)
    s_tree = lax.dot_general(group, keys, contract, preferred_element_type=F32) * scale
    mask = jnp.concatenate([anc_ref[...]] * heads, axis=0)
    s_tree = jnp.where(mask > 0, s_tree, NEG)
    top = jnp.maximum(
        jnp.max(s_cache, axis=1, keepdims=True), jnp.max(s_tree, axis=1, keepdims=True)
    )
    e_cache = jnp.exp(s_cache - top)
    e_tree = jnp.exp(s_tree - top)
    denominator = jnp.sum(e_cache, axis=1, keepdims=True) + jnp.sum(e_tree, axis=1, keepdims=True)
    weighted = jnp.dot(e_cache.astype(BF), vc_ref[...], preferred_element_type=F32)
    weighted = weighted + jnp.dot(e_tree.astype(BF), values, preferred_element_type=F32)
    ctx = (weighted / denominator).astype(BF)
    ctx = jnp.concatenate([ctx[h * nodes : (h + 1) * nodes] for h in range(heads)], axis=1)
    ctx_ref[...] = ctx
    for j in range(n_x):
        cols = pl.ds(pl.multiple_of(step(j, me ^ 1) * width, width), width)
        send_ref[j] = jnp.dot(ctx, wout_ref[:, cols], preferred_element_type=F32).astype(BF)


def spread_kernel(ids_ref, out_ref):
    out_ref[...] = jnp.broadcast_to(ids_ref[...], out_ref.shape)


def load_kernel(count, *refs):
    dst = refs[-1 - count : -1]
    copies = [pltpu.make_async_copy(refs[i], dst[i], refs[-1].at[i]) for i in range(count)]
    for copy in copies:
        copy.start()
    for copy in copies:
        copy.wait()


def load(arrays, after, mib):
    return pl.pallas_call(
        functools.partial(load_kernel, len(arrays)),
        out_shape=tuple(jax.ShapeDtypeStruct(a.shape, a.dtype) for a in arrays),
        in_specs=[pl.BlockSpec(memory_space=pltpu.HBM)] * len(arrays)
        + [pl.BlockSpec(memory_space=pl.ANY)] * len(after),
        out_specs=(pl.BlockSpec(memory_space=pltpu.VMEM),) * len(arrays),
        scratch_shapes=[pltpu.SemaphoreType.DMA((len(arrays),))],
        cost_estimate=pl.CostEstimate(
            flops=0, bytes_accessed=sum(a.size * a.dtype.itemsize for a in arrays), transcendentals=0
        ),
        compiler_params=limit(mib),
        name="load",
    )(*arrays, *after)


def out_kernel(idx_ref, ctx_ref, wout_ref, out_ref):
    n_x, _, width = out_ref.shape
    ctx = ctx_ref[...]
    for j in range(n_x):
        cols = pl.ds(pl.multiple_of(step(j, idx_ref[0]) * width, width), width)
        out_ref[j] = jnp.dot(ctx, wout_ref[:, cols], preferred_element_type=F32)


def pair_kernel(own_ref, came_ref, *out_refs):
    for j, ref in enumerate(out_refs):
        ref[...] = (own_ref[j] + came_ref[j].astype(F32)).astype(ref.dtype)


def stack_kernel(*refs):
    out_ref = refs[-1]
    for j in range(out_ref.shape[0]):
        out_ref[j] = refs[j][...]


def final_kernel(emb_ref, own_ref, *refs):
    total = own_ref[...]
    for ref in refs[:-1]:
        total = total + ref[...].astype(F32)
    refs[-1][...] = (emb_ref[...].astype(F32) + total).astype(BF)


def limit(mib):
    return pltpu.CompilerParams(vmem_limit_bytes=mib * 1024 * 1024)


def swap(n, k):
    return [(i, i ^ k) for i in range(n)]


def shards(tree_ids, ancestors, lengths, table, gain, w_query, w_kv, w_out, key_cache, value_cache):
    n_dp = lax.axis_size("dp")
    n_tp = lax.axis_size("tensor")
    n_x = n_tp // 2
    nodes = tree_ids.shape[1]
    vocab, width = table.shape
    me = lax.axis_index("tensor")
    me_arr = me.astype(jnp.int32).reshape(1)
    part = lax.axis_index("dp").astype(jnp.int32).reshape(1)
    vmem = pl.BlockSpec(memory_space=pltpu.VMEM)
    smem = pl.BlockSpec(memory_space=pltpu.SMEM)

    copies = pl.pallas_call(
        spread_kernel,
        out_shape=jax.ShapeDtypeStruct((n_dp, nodes), jnp.int32),
        in_specs=[vmem],
        out_specs=vmem,
        compiler_params=limit(60),
        name="spread",
    )(tree_ids)
    all_ids = lax.all_to_all(copies, "dp", split_axis=0, concat_axis=0, tiled=True)
    (table_held,) = load((table,), (), 50)
    rows = pl.pallas_call(
        rows_kernel,
        out_shape=jax.ShapeDtypeStruct((n_dp // 2, 2, 2 * CAP, width // 2), BF),
        in_specs=[smem, vmem, vmem],
        out_specs=vmem,
        compiler_params=limit(12),
        name="rows",
    )(part, all_ids, table_held)
    w_kv, key_cache, value_cache = load((w_kv, key_cache, value_cache), (rows,), 50)
    recv = lax.all_to_all(
        rows.reshape(n_dp, 2 * CAP, width // 2), "dp", split_axis=0, concat_axis=0, tiled=True
    )
    emb = pl.pallas_call(
        functools.partial(pick_kernel, vocab=vocab),
        out_shape=jax.ShapeDtypeStruct((nodes, width), BF),
        in_specs=[vmem, vmem, pl.BlockSpec(memory_space=pl.ANY)],
        out_specs=vmem,
        compiler_params=limit(4),
        name="pick",
    )(tree_ids, recv.reshape(n_dp * 2 * CAP, width // 2), w_kv)

    w_query, w_out = load((w_query, w_out), (emb,), 45)
    mine = pl.pallas_call(
        stack_kernel,
        in_specs=[vmem] * n_x + [pl.BlockSpec(memory_space=pl.ANY)],
        out_specs=vmem,
        out_shape=jax.ShapeDtypeStruct((n_x, nodes, width), BF),
        compiler_params=limit(4),
        name="stack",
    )(emb, *[lax.ppermute(emb, "tensor", [(i, step(j, i)) for i in range(n_tp)]) for j in range(1, n_x)], w_query)
    other = lax.ppermute(mine, "tensor", swap(n_tp, 1))

    depth = jnp.sum(ancestors[0], axis=1) - 1
    positions = (lengths[0] + depth).astype(F32)
    freq_index = jnp.arange(HD // 2, dtype=F32)
    inverse = jnp.exp(freq_index * (-2.0 * math.log(THETA) / HD))
    angles = positions[:, None] * inverse[None, :]
    cosine = jnp.cos(angles)
    sine = jnp.sin(angles)
    cos = jnp.concatenate([cosine, cosine], axis=1)
    sin = jnp.concatenate([-sine, sine], axis=1)

    ctx, send = pl.pallas_call(
        layer_kernel,
        out_shape=(
            jax.ShapeDtypeStruct((nodes, width), BF),
            jax.ShapeDtypeStruct((n_x, nodes, width), BF),
        ),
        in_specs=[smem, smem] + [vmem] * 11,
        out_specs=(vmem, vmem),
        scratch_shapes=[pltpu.VMEM((nodes, n_tp * width), BF)],
        compiler_params=limit(16),
        name="layer",
    )(
        me_arr, lengths, mine, other, gain.reshape(1, -1), w_query, w_kv, w_out,
        key_cache[0, 0], value_cache[0, 0], ancestors[0], cos, sin,
    )
    came = lax.ppermute(send, "tensor", swap(n_tp, 1))
    own = pl.pallas_call(
        out_kernel,
        in_specs=[smem, vmem, vmem],
        out_specs=vmem,
        out_shape=jax.ShapeDtypeStruct((n_x, nodes, width), F32),
        cost_estimate=pl.CostEstimate(
            flops=2 * nodes * width * width * n_x, bytes_accessed=2 * width * width * n_x, transcendentals=0
        ),
        compiler_params=limit(8),
        name="project",
    )(me_arr, ctx, w_out)
    pairs = pl.pallas_call(
        pair_kernel,
        in_specs=[vmem, vmem],
        out_specs=(vmem,) * n_x,
        out_shape=tuple(jax.ShapeDtypeStruct((nodes, width), F32 if j == 0 else BF) for j in range(n_x)),
        compiler_params=limit(4),
        name="pair",
    )(own, came)
    parts = [lax.ppermute(pairs[j], "tensor", [(i, step(j, i)) for i in range(n_tp)]) for j in range(1, n_x)]
    return pl.pallas_call(
        final_kernel,
        in_specs=[vmem] * (n_x + 1),
        out_specs=vmem,
        out_shape=jax.ShapeDtypeStruct((nodes, width), BF),
        compiler_params=limit(4),
        name="final",
    )(emb, pairs[0], *parts)


def solution(mesh):
    in_specs = (
        P("dp", None),
        P("dp", None, None),
        P("dp"),
        P("dp", "tensor"),
        P(),
        P(None, "tensor"),
        P(None, None, "tensor"),
        P("tensor", None),
        P("dp", "tensor", None, None),
        P("dp", "tensor", None, None),
    )
    out_specs = P("dp", "tensor")
    return jax.shard_map(shards, mesh=mesh, in_specs=in_specs, out_specs=out_specs, check_vma=False)
```

```python
import functools
import math

import jax
import jax.numpy as jnp
from jax import lax
from jax.experimental import pallas as pl
from jax.experimental.pallas import tpu as pltpu
from jax.sharding import PartitionSpec as P

D = 4096
HD = 128
CAP = 4
EPS = 1e-05
NEG = -1e30
THETA = 500000.0
BF = jnp.bfloat16
F32 = jnp.float32


def iota(shape, dim):
    return lax.broadcasted_iota(jnp.int32, shape, dim)


def rows_kernel(idx_ref, ids_ref, table_ref, _, out_ref):
    vocab = table_ref.shape[0]
    n_dst, nodes = ids_ref.shape
    off = ids_ref[...] - idx_ref[0] * vocab
    owned = (off >= 0) & (off < vocab)
    before = jnp.where(iota((nodes, nodes), 0) < iota((nodes, nodes), 1), 1.0, 0.0).astype(BF)
    rank = jnp.dot(jnp.where(owned, 1.0, 0.0).astype(BF), before, preferred_element_type=F32)
    high = jnp.where(owned, rank * (vocab // 256) + (off >> 8).astype(F32), -1.0).astype(BF)
    low = jnp.where(owned, (off & 255).astype(F32), 0.0).astype(BF)
    n_out = n_dst * CAP
    spread = jnp.where(
        iota((n_out, n_dst), 0) // CAP == iota((n_out, n_dst), 1), 1.0, 0.0
    ).astype(BF)
    code = 256.0 * jnp.dot(spread, high, preferred_element_type=F32) + jnp.dot(
        spread, low, preferred_element_type=F32
    )
    code = code.astype(jnp.int32)
    slot = (iota((n_out, nodes), 0) & (CAP - 1)) * vocab
    rel = code - slot
    entry = jnp.max(
        jnp.where((rel >= 0) & (rel < vocab), rel, -1).astype(F32), axis=1, keepdims=True
    ).astype(jnp.int32)
    pick = jnp.where(iota((n_out, vocab), 1) == entry, 1.0, 0.0).astype(BF)
    rows = jnp.dot(pick, table_ref[...], preferred_element_type=F32)
    half = rows.shape[1] // 2
    low_half = rows[:, :half].reshape(n_dst // 2, 2 * CAP, half)
    high_half = rows[:, half:].reshape(n_dst // 2, 2 * CAP, half)
    first = iota(low_half.shape, 1) < CAP
    out_ref[:, 0] = jnp.where(first, low_half, pltpu.roll(high_half, CAP, 1)).astype(BF)
    out_ref[:, 1] = jnp.where(first, pltpu.roll(low_half, CAP, 1), high_half).astype(BF)


def pick_kernel(ids_ref, recv_ref, out_ref, *, vocab):
    nodes = ids_ref.shape[1]
    n_in, half = recv_ref.shape
    ids_row = jnp.broadcast_to(ids_ref[...], (nodes, nodes)) // vocab
    owner_row = ids_row.astype(F32)
    owner_col = owner_row.T
    same = (owner_row == owner_col) & (iota((nodes, nodes), 1) < iota((nodes, nodes), 0))
    rank = jnp.sum(jnp.where(same, 1.0, 0.0), axis=1, keepdims=True)
    slot = (owner_col[:, 0:1] * 8.0 + rank).astype(jnp.int32)
    columns = iota((nodes, n_in), 1)
    recv = recv_ref[...]
    low = jnp.where(columns == slot, 1.0, 0.0).astype(BF)
    high = jnp.where(columns == slot + CAP, 1.0, 0.0).astype(BF)
    out_ref[:, :half] = jnp.dot(low, recv, preferred_element_type=F32).astype(BF)
    out_ref[:, half:] = jnp.dot(high, recv, preferred_element_type=F32).astype(BF)


def step(j, device):
    core = device & 1
    return device ^ (0, 2 + 2 * core, 4 + 2 * core, 6 - 4 * core)[j]


def live_kernel(len_ref, out_ref):
    out_ref[...] = jnp.full(out_ref.shape, len_ref[0], jnp.int32)


def place_kernel(len_ref, anc_ref, _, out_ref):
    depth = jnp.sum(anc_ref[...].astype(F32), axis=1, keepdims=True).astype(jnp.int32) - 1
    out_ref[...] = jnp.broadcast_to((len_ref[:, 0:1] + depth).astype(F32), out_ref.shape)


def rotate(x, cos, sin):
    return x * cos + pltpu.roll(x, HD // 2, 1) * sin


def layer_kernel(
    len_ref, mine_ref, other_ref, gain_ref, wq_ref, wkv_ref, wout_ref, kc_ref, vc_ref,
    anc_ref, cos_ref, sin_ref, ctx_ref, send_ref, normed,
):
    me = lax.axis_index("tensor")
    n_x, nodes, width = mine_ref.shape
    total = jnp.zeros((nodes, 1), F32)
    for j in range(n_x):
        for ref in (mine_ref, other_ref):
            piece = ref[j].astype(F32)
            total = total + jnp.sum(piece * piece, axis=1, keepdims=True)
    inv_rms = lax.rsqrt(total / D + EPS)
    for j in range(n_x):
        for c, ref in enumerate((mine_ref, other_ref)):
            owner = step(j, me ^ c)
            cols = pl.ds(pl.multiple_of(owner * width, width), width)
            gain = gain_ref[:, cols].astype(F32)
            normed[:, cols] = (ref[j].astype(F32) * inv_rms * gain).astype(BF)
    x = normed[...]
    queries = jnp.dot(x, wq_ref[...], preferred_element_type=F32)
    keys = jnp.dot(x, wkv_ref[0], preferred_element_type=F32)
    values = jnp.dot(x, wkv_ref[1], preferred_element_type=F32).astype(BF)
    cos = cos_ref[...]
    sin = sin_ref[...]
    heads = queries.shape[1] // HD
    keys = rotate(keys, cos, sin).astype(BF)
    group = jnp.concatenate(
        [rotate(queries[:, h * HD : (h + 1) * HD], cos, sin).astype(BF) for h in range(heads)], axis=0
    )
    contract = (((1,), (1,)), ((), ()))
    scale = HD ** (-0.5)
    slots = kc_ref.shape[0]
    s_cache = lax.dot_general(group, kc_ref[...], contract, preferred_element_type=F32) * scale
    s_cache = jnp.where(iota((1, slots), 1) < len_ref[:, 0:1], s_cache, NEG)
    s_tree = lax.dot_general(group, keys, contract, preferred_element_type=F32) * scale
    mask = jnp.concatenate([anc_ref[...]] * heads, axis=0)
    s_tree = jnp.where(mask > 0, s_tree, NEG)
    top = jnp.maximum(
        jnp.max(s_cache, axis=1, keepdims=True), jnp.max(s_tree, axis=1, keepdims=True)
    )
    e_cache = jnp.exp(s_cache - top)
    e_tree = jnp.exp(s_tree - top)
    denominator = jnp.sum(e_cache, axis=1, keepdims=True) + jnp.sum(e_tree, axis=1, keepdims=True)
    weighted = jnp.dot(e_cache.astype(BF), vc_ref[...], preferred_element_type=F32)
    weighted = weighted + jnp.dot(e_tree.astype(BF), values, preferred_element_type=F32)
    ctx = (weighted / denominator).astype(BF)
    ctx = jnp.concatenate([ctx[h * nodes : (h + 1) * nodes] for h in range(heads)], axis=1)
    ctx_ref[...] = ctx
    for j in range(n_x):
        cols = pl.ds(pl.multiple_of(step(j, me ^ 1) * width, width), width)
        send_ref[j] = jnp.dot(ctx, wout_ref[:, cols], preferred_element_type=F32).astype(BF)


def spread_kernel(ids_ref, out_ref):
    out_ref[...] = jnp.broadcast_to(ids_ref[...], out_ref.shape)


def load_kernel(count, *refs):
    dst = refs[-1 - count : -1]
    copies = [pltpu.make_async_copy(refs[i], dst[i], refs[-1].at[i]) for i in range(count)]
    for copy in copies:
        copy.start()
    for copy in copies:
        copy.wait()


def load(arrays, after, mib):
    return pl.pallas_call(
        functools.partial(load_kernel, len(arrays)),
        out_shape=tuple(jax.ShapeDtypeStruct(a.shape, a.dtype) for a in arrays),
        in_specs=[pl.BlockSpec(memory_space=pltpu.HBM)] * len(arrays)
        + [pl.BlockSpec(memory_space=pl.ANY)] * len(after),
        out_specs=(pl.BlockSpec(memory_space=pltpu.VMEM),) * len(arrays),
        scratch_shapes=[pltpu.SemaphoreType.DMA((len(arrays),))],
        cost_estimate=pl.CostEstimate(
            flops=0, bytes_accessed=sum(a.size * a.dtype.itemsize for a in arrays), transcendentals=0
        ),
        compiler_params=limit(mib),
        name="load",
    )(*arrays, *after)


def out_kernel(ctx_ref, wout_ref, out_ref):
    n_x, _, width = out_ref.shape
    ctx = ctx_ref[...]
    for j in range(n_x):
        cols = pl.ds(pl.multiple_of(step(j, lax.axis_index("tensor")) * width, width), width)
        out_ref[j] = jnp.dot(ctx, wout_ref[:, cols], preferred_element_type=F32)


def pair_kernel(own_ref, came_ref, *out_refs):
    for j, ref in enumerate(out_refs):
        ref[...] = (own_ref[j] + came_ref[j].astype(F32)).astype(ref.dtype)


def stack_kernel(*refs):
    out_ref = refs[-1]
    for j in range(out_ref.shape[0]):
        out_ref[j] = refs[j][...]


def final_kernel(emb_ref, own_ref, *refs):
    total = own_ref[...]
    for ref in refs[:-1]:
        total = total + ref[...].astype(F32)
    refs[-1][...] = (emb_ref[...].astype(F32) + total).astype(BF)


def limit(mib):
    return pltpu.CompilerParams(vmem_limit_bytes=mib * 1024 * 1024)


def swap(n, k):
    return [(i, i ^ k) for i in range(n)]


def shards(tree_ids, ancestors, lengths, table, gain, w_query, w_kv, w_out, key_cache, value_cache):
    n_dp = lax.axis_size("dp")
    n_tp = lax.axis_size("tensor")
    n_x = n_tp // 2
    nodes = tree_ids.shape[1]
    vocab, width = table.shape
    part = lax.axis_index("dp").astype(jnp.int32).reshape(1)
    vmem = pl.BlockSpec(memory_space=pltpu.VMEM)
    smem = pl.BlockSpec(memory_space=pltpu.SMEM)

    copies = pl.pallas_call(
        spread_kernel,
        out_shape=jax.ShapeDtypeStruct((n_dp, nodes), jnp.int32),
        in_specs=[vmem],
        out_specs=vmem,
        compiler_params=limit(60),
        name="spread",
    )(tree_ids)
    all_ids = lax.all_to_all(copies, "dp", split_axis=0, concat_axis=0, tiled=True)
    live = pl.pallas_call(
        live_kernel,
        out_shape=jax.ShapeDtypeStruct((1, HD), jnp.int32),
        in_specs=[smem],
        out_specs=vmem,
        compiler_params=limit(4),
        name="live",
    )(lengths)
    (table_held,) = load((table,), (), 50)
    rows = pl.pallas_call(
        rows_kernel,
        out_shape=jax.ShapeDtypeStruct((n_dp // 2, 2, 2 * CAP, width // 2), BF),
        in_specs=[smem, vmem, vmem, pl.BlockSpec(memory_space=pl.ANY)],
        out_specs=vmem,
        compiler_params=limit(12),
        name="rows",
    )(part, all_ids, table_held, live)
    recv = lax.all_to_all(
        rows.reshape(n_dp, 2 * CAP, width // 2), "dp", split_axis=0, concat_axis=0, tiled=True
    )
    emb = pl.pallas_call(
        functools.partial(pick_kernel, vocab=vocab),
        out_shape=jax.ShapeDtypeStruct((nodes, width), BF),
        in_specs=[vmem, vmem],
        out_specs=vmem,
        compiler_params=limit(4),
        name="pick",
    )(tree_ids, recv.reshape(n_dp * 2 * CAP, width // 2))

    gain, emb = lax.optimization_barrier((gain, emb))
    w_query, w_out = load((w_query, w_out), (emb,), 45)
    mine = pl.pallas_call(
        stack_kernel,
        in_specs=[vmem] * n_x + [pl.BlockSpec(memory_space=pl.ANY)],
        out_specs=vmem,
        out_shape=jax.ShapeDtypeStruct((n_x, nodes, width), BF),
        compiler_params=limit(4),
        name="stack",
    )(emb, *[lax.ppermute(emb, "tensor", [(i, step(j, i)) for i in range(n_tp)]) for j in range(1, n_x)], w_query)
    other = lax.ppermute(mine, "tensor", swap(n_tp, 1))

    positions = pl.pallas_call(
        place_kernel,
        out_shape=jax.ShapeDtypeStruct((nodes, HD // 2), F32),
        in_specs=[vmem, vmem, pl.BlockSpec(memory_space=pl.ANY)],
        out_specs=vmem,
        compiler_params=limit(4),
        name="place",
    )(live, ancestors[0], emb)
    freq_index = jnp.arange(HD // 2, dtype=F32)
    inverse = jnp.exp(freq_index * (-2.0 * math.log(THETA) / HD))
    angles = positions * inverse[None, :]
    cosine = jnp.cos(angles)
    sine = jnp.sin(angles)
    cos = jnp.concatenate([cosine, cosine], axis=1)
    sin = jnp.concatenate([-sine, sine], axis=1)

    ctx, send = pl.pallas_call(
        layer_kernel,
        out_shape=(
            jax.ShapeDtypeStruct((nodes, width), BF),
            jax.ShapeDtypeStruct((n_x, nodes, width), BF),
        ),
        in_specs=[vmem] * 12,
        out_specs=(vmem, vmem),
        scratch_shapes=[pltpu.VMEM((nodes, n_tp * width), BF)],
        compiler_params=limit(16),
        name="layer",
    )(
        live, mine, other, gain.reshape(1, -1), w_query, w_kv, w_out,
        key_cache[0, 0], value_cache[0, 0], ancestors[0], cos, sin,
    )
    came = lax.ppermute(send, "tensor", swap(n_tp, 1))
    own = pl.pallas_call(
        out_kernel,
        in_specs=[vmem, vmem],
        out_specs=vmem,
        out_shape=jax.ShapeDtypeStruct((n_x, nodes, width), F32),
        cost_estimate=pl.CostEstimate(
            flops=2 * nodes * width * width * n_x, bytes_accessed=2 * width * width * n_x, transcendentals=0
        ),
        compiler_params=limit(8),
        name="project",
    )(ctx, w_out)
    pairs = pl.pallas_call(
        pair_kernel,
        in_specs=[vmem, vmem],
        out_specs=(vmem,) * n_x,
        out_shape=tuple(jax.ShapeDtypeStruct((nodes, width), F32 if j == 0 else BF) for j in range(n_x)),
        compiler_params=limit(4),
        name="pair",
    )(own, came)
    parts = [lax.ppermute(pairs[j], "tensor", [(i, step(j, i)) for i in range(n_tp)]) for j in range(1, n_x)]
    return pl.pallas_call(
        final_kernel,
        in_specs=[vmem] * (n_x + 1),
        out_specs=vmem,
        out_shape=jax.ShapeDtypeStruct((nodes, width), BF),
        compiler_params=limit(4),
        name="final",
    )(emb, pairs[0], *parts)


def solution(mesh):
    in_specs = (
        P("dp", None),
        P("dp", None, None),
        P("dp"),
        P("dp", "tensor"),
        P(),
        P(None, "tensor"),
        P(None, None, "tensor"),
        P("tensor", None),
        P("dp", "tensor", None, None),
        P("dp", "tensor", None, None),
    )
    out_specs = P("dp", "tensor")
    return jax.shard_map(shards, mesh=mesh, in_specs=in_specs, out_specs=out_specs, check_vma=False)
```

```python
import functools
import math

import jax
import jax.numpy as jnp
from jax import lax
from jax.experimental import pallas as pl
from jax.experimental.pallas import tpu as pltpu
from jax.sharding import PartitionSpec as P

D = 4096
HD = 128
CAP = 4
EPS = 1e-05
NEG = -1e30
THETA = 500000.0
BF = jnp.bfloat16
F32 = jnp.float32


def iota(shape, dim):
    return lax.broadcasted_iota(jnp.int32, shape, dim)


def rows_kernel(idx_ref, ids_ref, table_ref, _, out_ref):
    vocab = table_ref.shape[0]
    n_dst, nodes = ids_ref.shape
    off = ids_ref[...] - idx_ref[0] * vocab
    owned = (off >= 0) & (off < vocab)
    before = jnp.where(iota((nodes, nodes), 0) < iota((nodes, nodes), 1), 1.0, 0.0).astype(BF)
    rank = jnp.dot(jnp.where(owned, 1.0, 0.0).astype(BF), before, preferred_element_type=F32)
    high = jnp.where(owned, rank * (vocab // 256) + (off >> 8).astype(F32), -1.0).astype(BF)
    low = jnp.where(owned, (off & 255).astype(F32), 0.0).astype(BF)
    n_out = n_dst * CAP
    spread = jnp.where(
        iota((n_out, n_dst), 0) // CAP == iota((n_out, n_dst), 1), 1.0, 0.0
    ).astype(BF)
    code = 256.0 * jnp.dot(spread, high, preferred_element_type=F32) + jnp.dot(
        spread, low, preferred_element_type=F32
    )
    code = code.astype(jnp.int32)
    slot = (iota((n_out, nodes), 0) & (CAP - 1)) * vocab
    rel = code - slot
    entry = jnp.max(
        jnp.where((rel >= 0) & (rel < vocab), rel, -1).astype(F32), axis=1, keepdims=True
    ).astype(jnp.int32)
    pick = jnp.where(iota((n_out, vocab), 1) == entry, 1.0, 0.0).astype(BF)
    rows = jnp.dot(pick, table_ref[...], preferred_element_type=F32)
    half = rows.shape[1] // 2
    low_half = rows[:, :half].reshape(n_dst // 2, 2 * CAP, half)
    high_half = rows[:, half:].reshape(n_dst // 2, 2 * CAP, half)
    first = iota(low_half.shape, 1) < CAP
    out_ref[:, 0] = jnp.where(first, low_half, pltpu.roll(high_half, CAP, 1)).astype(BF)
    out_ref[:, 1] = jnp.where(first, pltpu.roll(low_half, CAP, 1), high_half).astype(BF)


def pick_kernel(ids_ref, recv_ref, out_ref, *, vocab):
    nodes = ids_ref.shape[1]
    n_in, half = recv_ref.shape
    ids_row = jnp.broadcast_to(ids_ref[...], (nodes, nodes)) // vocab
    owner_row = ids_row.astype(F32)
    owner_col = owner_row.T
    same = (owner_row == owner_col) & (iota((nodes, nodes), 1) < iota((nodes, nodes), 0))
    rank = jnp.sum(jnp.where(same, 1.0, 0.0), axis=1, keepdims=True)
    slot = (owner_col[:, 0:1] * 8.0 + rank).astype(jnp.int32)
    columns = iota((nodes, n_in), 1)
    recv = recv_ref[...]
    low = jnp.where(columns == slot, 1.0, 0.0).astype(BF)
    high = jnp.where(columns == slot + CAP, 1.0, 0.0).astype(BF)
    out_ref[:, :half] = jnp.dot(low, recv, preferred_element_type=F32).astype(BF)
    out_ref[:, half:] = jnp.dot(high, recv, preferred_element_type=F32).astype(BF)


def step(j, device):
    core = device & 1
    return device ^ (0, 2 + 4 * core, 4, 6 - 4 * core)[j]


def live_kernel(len_ref, out_ref):
    out_ref[...] = jnp.full(out_ref.shape, len_ref[0], jnp.int32)


def place_kernel(len_ref, anc_ref, _, out_ref):
    depth = jnp.sum(anc_ref[...].astype(F32), axis=1, keepdims=True).astype(jnp.int32) - 1
    out_ref[...] = jnp.broadcast_to((len_ref[:, 0:1] + depth).astype(F32), out_ref.shape)


def rotate(x, cos, sin):
    return x * cos + pltpu.roll(x, HD // 2, 1) * sin


def layer_kernel(
    len_ref, mine_ref, other_ref, gain_ref, wq_ref, wkv_ref, wout_ref, kc_ref, vc_ref,
    anc_ref, cos_ref, sin_ref, ctx_ref, send_ref, normed,
):
    me = lax.axis_index("tensor")
    n_x, nodes, width = mine_ref.shape
    total = jnp.zeros((nodes, 1), F32)
    for j in range(n_x):
        for ref in (mine_ref, other_ref):
            piece = ref[j].astype(F32)
            total = total + jnp.sum(piece * piece, axis=1, keepdims=True)
    inv_rms = lax.rsqrt(total / D + EPS)
    for j in range(n_x):
        for c, ref in enumerate((mine_ref, other_ref)):
            owner = step(j, me ^ c)
            cols = pl.ds(pl.multiple_of(owner * width, width), width)
            gain = gain_ref[:, cols].astype(F32)
            normed[:, cols] = (ref[j].astype(F32) * inv_rms * gain).astype(BF)
    x = normed[...]
    queries = jnp.dot(x, wq_ref[...], preferred_element_type=F32)
    keys = jnp.dot(x, wkv_ref[0], preferred_element_type=F32)
    values = jnp.dot(x, wkv_ref[1], preferred_element_type=F32).astype(BF)
    cos = cos_ref[...]
    sin = sin_ref[...]
    heads = queries.shape[1] // HD
    keys = rotate(keys, cos, sin).astype(BF)
    group = jnp.concatenate(
        [rotate(queries[:, h * HD : (h + 1) * HD], cos, sin).astype(BF) for h in range(heads)], axis=0
    )
    contract = (((1,), (1,)), ((), ()))
    scale = HD ** (-0.5)
    slots = kc_ref.shape[0]
    s_cache = lax.dot_general(group, kc_ref[...], contract, preferred_element_type=F32) * scale
    s_cache = jnp.where(iota((1, slots), 1) < len_ref[:, 0:1], s_cache, NEG)
    s_tree = lax.dot_general(group, keys, contract, preferred_element_type=F32) * scale
    mask = jnp.concatenate([anc_ref[...]] * heads, axis=0)
    s_tree = jnp.where(mask > 0, s_tree, NEG)
    top = jnp.maximum(
        jnp.max(s_cache, axis=1, keepdims=True), jnp.max(s_tree, axis=1, keepdims=True)
    )
    e_cache = jnp.exp(s_cache - top)
    e_tree = jnp.exp(s_tree - top)
    denominator = jnp.sum(e_cache, axis=1, keepdims=True) + jnp.sum(e_tree, axis=1, keepdims=True)
    weighted = jnp.dot(e_cache.astype(BF), vc_ref[...], preferred_element_type=F32)
    weighted = weighted + jnp.dot(e_tree.astype(BF), values, preferred_element_type=F32)
    ctx = (weighted / denominator).astype(BF)
    ctx = jnp.concatenate([ctx[h * nodes : (h + 1) * nodes] for h in range(heads)], axis=1)
    ctx_ref[...] = ctx
    for j in range(n_x):
        cols = pl.ds(pl.multiple_of(step(j, me ^ 1) * width, width), width)
        send_ref[j] = jnp.dot(ctx, wout_ref[:, cols], preferred_element_type=F32).astype(BF)


def spread_kernel(ids_ref, out_ref):
    out_ref[...] = jnp.broadcast_to(ids_ref[...], out_ref.shape)


def load_kernel(count, *refs):
    dst = refs[-1 - count : -1]
    copies = [pltpu.make_async_copy(refs[i], dst[i], refs[-1].at[i]) for i in range(count)]
    for copy in copies:
        copy.start()
    for copy in copies:
        copy.wait()


def load(arrays, after, mib):
    return pl.pallas_call(
        functools.partial(load_kernel, len(arrays)),
        out_shape=tuple(jax.ShapeDtypeStruct(a.shape, a.dtype) for a in arrays),
        in_specs=[pl.BlockSpec(memory_space=pltpu.HBM)] * len(arrays)
        + [pl.BlockSpec(memory_space=pl.ANY)] * len(after),
        out_specs=(pl.BlockSpec(memory_space=pltpu.VMEM),) * len(arrays),
        scratch_shapes=[pltpu.SemaphoreType.DMA((len(arrays),))],
        cost_estimate=pl.CostEstimate(
            flops=0, bytes_accessed=sum(a.size * a.dtype.itemsize for a in arrays), transcendentals=0
        ),
        compiler_params=limit(mib),
        name="load",
    )(*arrays, *after)


def out_kernel(ctx_ref, wout_ref, out_ref):
    n_x, _, width = out_ref.shape
    ctx = ctx_ref[...]
    for j in range(n_x):
        cols = pl.ds(pl.multiple_of(step(j, lax.axis_index("tensor")) * width, width), width)
        out_ref[j] = jnp.dot(ctx, wout_ref[:, cols], preferred_element_type=F32)


def pair_kernel(own_ref, came_ref, *out_refs):
    for j, ref in enumerate(out_refs):
        ref[...] = (own_ref[j] + came_ref[j].astype(F32)).astype(ref.dtype)


def stack_kernel(*refs):
    out_ref = refs[-1]
    for j in range(out_ref.shape[0]):
        out_ref[j] = refs[j][...]


def final_kernel(emb_ref, own_ref, *refs):
    total = own_ref[...]
    for ref in refs[:-1]:
        total = total + ref[...].astype(F32)
    refs[-1][...] = (emb_ref[...].astype(F32) + total).astype(BF)


def limit(mib):
    return pltpu.CompilerParams(vmem_limit_bytes=mib * 1024 * 1024)


def swap(n, k):
    return [(i, i ^ k) for i in range(n)]


def shards(tree_ids, ancestors, lengths, table, gain, w_query, w_kv, w_out, key_cache, value_cache):
    n_dp = lax.axis_size("dp")
    n_tp = lax.axis_size("tensor")
    n_x = n_tp // 2
    nodes = tree_ids.shape[1]
    vocab, width = table.shape
    part = lax.axis_index("dp").astype(jnp.int32).reshape(1)
    vmem = pl.BlockSpec(memory_space=pltpu.VMEM)
    smem = pl.BlockSpec(memory_space=pltpu.SMEM)

    copies = pl.pallas_call(
        spread_kernel,
        out_shape=jax.ShapeDtypeStruct((n_dp, nodes), jnp.int32),
        in_specs=[vmem],
        out_specs=vmem,
        compiler_params=limit(60),
        name="spread",
    )(tree_ids)
    all_ids = lax.all_to_all(copies, "dp", split_axis=0, concat_axis=0, tiled=True)
    live = pl.pallas_call(
        live_kernel,
        out_shape=jax.ShapeDtypeStruct((1, HD), jnp.int32),
        in_specs=[smem],
        out_specs=vmem,
        compiler_params=limit(4),
        name="live",
    )(lengths)
    (table_held,) = load((table,), (), 50)
    rows = pl.pallas_call(
        rows_kernel,
        out_shape=jax.ShapeDtypeStruct((n_dp // 2, 2, 2 * CAP, width // 2), BF),
        in_specs=[smem, vmem, vmem, pl.BlockSpec(memory_space=pl.ANY)],
        out_specs=vmem,
        compiler_params=limit(12),
        name="rows",
    )(part, all_ids, table_held, live)
    recv = lax.all_to_all(
        rows.reshape(n_dp, 2 * CAP, width // 2), "dp", split_axis=0, concat_axis=0, tiled=True
    )
    emb = pl.pallas_call(
        functools.partial(pick_kernel, vocab=vocab),
        out_shape=jax.ShapeDtypeStruct((nodes, width), BF),
        in_specs=[vmem, vmem],
        out_specs=vmem,
        compiler_params=limit(4),
        name="pick",
    )(tree_ids, recv.reshape(n_dp * 2 * CAP, width // 2))

    gain, emb = lax.optimization_barrier((gain, emb))
    w_query, w_out = load((w_query, w_out), (emb,), 45)
    mine = pl.pallas_call(
        stack_kernel,
        in_specs=[vmem] * n_x + [pl.BlockSpec(memory_space=pl.ANY)],
        out_specs=vmem,
        out_shape=jax.ShapeDtypeStruct((n_x, nodes, width), BF),
        compiler_params=limit(4),
        name="stack",
    )(emb, *[lax.ppermute(emb, "tensor", [(i, step(j, i)) for i in range(n_tp)]) for j in range(1, n_x)], w_query)
    other = lax.ppermute(mine, "tensor", swap(n_tp, 1))

    positions = pl.pallas_call(
        place_kernel,
        out_shape=jax.ShapeDtypeStruct((nodes, HD // 2), F32),
        in_specs=[vmem, vmem, pl.BlockSpec(memory_space=pl.ANY)],
        out_specs=vmem,
        compiler_params=limit(4),
        name="place",
    )(live, ancestors[0], emb)
    freq_index = jnp.arange(HD // 2, dtype=F32)
    inverse = jnp.exp(freq_index * (-2.0 * math.log(THETA) / HD))
    angles = positions * inverse[None, :]
    cosine = jnp.cos(angles)
    sine = jnp.sin(angles)
    cos = jnp.concatenate([cosine, cosine], axis=1)
    sin = jnp.concatenate([-sine, sine], axis=1)

    ctx, send = pl.pallas_call(
        layer_kernel,
        out_shape=(
            jax.ShapeDtypeStruct((nodes, width), BF),
            jax.ShapeDtypeStruct((n_x, nodes, width), BF),
        ),
        in_specs=[vmem] * 12,
        out_specs=(vmem, vmem),
        scratch_shapes=[pltpu.VMEM((nodes, n_tp * width), BF)],
        compiler_params=limit(16),
        name="layer",
    )(
        live, mine, other, gain.reshape(1, -1), w_query, w_kv, w_out,
        key_cache[0, 0], value_cache[0, 0], ancestors[0], cos, sin,
    )
    came = lax.ppermute(send, "tensor", swap(n_tp, 1))
    own = pl.pallas_call(
        out_kernel,
        in_specs=[vmem, vmem],
        out_specs=vmem,
        out_shape=jax.ShapeDtypeStruct((n_x, nodes, width), F32),
        cost_estimate=pl.CostEstimate(
            flops=2 * nodes * width * width * n_x, bytes_accessed=2 * width * width * n_x, transcendentals=0
        ),
        compiler_params=limit(8),
        name="project",
    )(ctx, w_out)
    pairs = pl.pallas_call(
        pair_kernel,
        in_specs=[vmem, vmem],
        out_specs=(vmem,) * n_x,
        out_shape=tuple(jax.ShapeDtypeStruct((nodes, width), F32 if j == 0 else BF) for j in range(n_x)),
        compiler_params=limit(4),
        name="pair",
    )(own, came)
    parts = [lax.ppermute(pairs[j], "tensor", [(i, step(j, i)) for i in range(n_tp)]) for j in range(1, n_x)]
    return pl.pallas_call(
        final_kernel,
        in_specs=[vmem] * (n_x + 1),
        out_specs=vmem,
        out_shape=jax.ShapeDtypeStruct((nodes, width), BF),
        compiler_params=limit(4),
        name="final",
    )(emb, pairs[0], *parts)


def solution(mesh):
    in_specs = (
        P("dp", None),
        P("dp", None, None),
        P("dp"),
        P("dp", "tensor"),
        P(),
        P(None, "tensor"),
        P(None, None, "tensor"),
        P("tensor", None),
        P("dp", "tensor", None, None),
        P("dp", "tensor", None, None),
    )
    out_specs = P("dp", "tensor")
    return jax.shard_map(shards, mesh=mesh, in_specs=in_specs, out_specs=out_specs, check_vma=False)
```
